256 devices in a mesh: queue: 16 (over z_lo, x, core), head: 16 (over y, z_hi).
Axes of the slice: x: 4, y: 4, z: 8 (z_hi: 4, z_lo: 2; z = z_hi * 2 + z_lo), core: 2. Of those that a mesh axis runs over, the one named last changes fastest.
Arguments:
- queries: bfloat16 [32768, 4096], P(('queue', 'head'))
- key_proj: bfloat16 [32768, 4096], P(('queue', 'head'))
- value_proj: bfloat16 [32768, 4096], P(('queue', 'head')), may hold values from -6 to 6
- residual: bfloat16 [32768, 4096], P(('queue', 'head')), may hold values from -6 to 6
- query_gain: float32 [4096], replicated, may hold values from 1 to 3
- key_gain: float32 [4096], replicated, may hold values from 1 to 3
- gate_table: float32 [50, 4096], replicated, may hold values from -6 to 6
- noise_level: int32 [64], replicated, may hold values from 0 to 49
- frame_reach: int32 [64], replicated, may hold values from 1 to 4, as said below
Outputs:
- advanced: bfloat16 [32768, 4096], P(('queue', 'head'))
- key_cache: bfloat16 [32768, 4096], P(('queue', 'head'))
- value_cache: bfloat16 [32768, 4096], P(('queue', 'head'))
The draws below stay inside these ranges and needn't reach their ends.
Inputs may be any that keep to these rules, and one draw needn't show every extreme that they name: `frame_reach`: both 1 and 4 occur among the values.
All inputs are finite; a program needn't handle non-finite values.
Results may differ from the reference program's by a relative error of at most 0.012.
The reference program's roundings to bfloat16 on the way (of `query_norm`, `key_norm`, `weights` and `attention`) count: a program that leaves them out, or rounds other values in their place, can miss the bound.
Values may be sent and summed in bfloat16 or wider, within the bound.
No kernel may reach another device: no remote copies, remote signals or barrier semaphores. Data moves between devices by JAX's collectives and lax.ppermute only.
A program may use at most 128 MiB of HBM per device.

```python
import math
import jax
import jax.numpy as jnp
from jax import lax

HD = 128
FRAMES_GRP = 4
LEVELS = 50
HEADS = 32
FEATS = 4096
GROUP_TOK = 2048
FRAME_TOK = 512
FRAMES = 64
TOKENS = 32768
N_QUEUE = 16


def draw_queries(key, part):
    key = jax.random.fold_in(key, 1)
    key_base, key_row = jax.random.split(key, 2)
    base = jax.random.normal(key_base, (TOKENS, FEATS), jnp.float32)
    row_scale = jnp.exp(jax.random.uniform(key_row, (TOKENS, 1), jnp.float32, 0.0, math.log(10.0)))
    return (base * row_scale).astype(jnp.bfloat16)


def draw_key_proj(key, part):
    key = jax.random.fold_in(key, 2)
    key_base, key_row = jax.random.split(key, 2)
    base = jax.random.normal(key_base, (TOKENS, FEATS), jnp.float32)
    row_scale = jnp.exp(jax.random.uniform(key_row, (TOKENS, 1), jnp.float32, 0.0, math.log(10.0)))
    return (base * row_scale).astype(jnp.bfloat16)


def draw_frame_reach(key, part):
    key = jax.random.fold_in(key, 3)
    key_val, key_at, key_gap = jax.random.split(key, 3)
    reach_all = jax.random.randint(key_val, (FRAMES,), 1, FRAMES_GRP + 1)
    at_top = jax.random.randint(key_at, (), 0, FRAMES)
    at_low = (at_top + 1 + jax.random.randint(key_gap, (), 0, FRAMES - 1)) % FRAMES
    reach_all = reach_all.at[at_top].set(FRAMES_GRP)
    reach_all = reach_all.at[at_low].set(1)
    return reach_all.astype(jnp.int32)


def with_ends(result, stream_key, smallest, largest):
    longest = result.shape.index(max(result.shape))
    spots = []
    for shift in (0, 1):
        where = [jax.random.randint(jax.random.fold_in(stream_key, axis), (), 0, length) for axis, length in enumerate(result.shape)]
        where[longest] = (where[longest] + shift) % result.shape[longest]
        spots.append(tuple(where))
    return result.at[spots[0]].set(smallest).at[spots[1]].set(largest)


def block_scale(rng, dims, shards, smallest, top_value):
    level, own = 1.0, jax.random.fold_in(rng, 6)
    for dim, shards_of in shards:
        heights = jnp.exp(jax.random.uniform(jax.random.fold_in(own, dim), (shards_of,), jnp.float32, smallest / len(shards), top_value / len(shards)))
        level = level * jnp.repeat(heights, dims[dim] // shards_of).reshape([-1 if axis == dim else 1 for axis in range(len(dims))])
    return level


def noise(key, dims, width, bound, cuts=(), held_as=jnp.bfloat16):
    array = width * jax.random.normal(key, dims, jnp.float32)
    if cuts:
        array = array * block_scale(key, dims, cuts, -0.22, 0.18)
    return jnp.clip(array, -bound, bound).astype(held_as)


def setup_inputs(seed: int = 0) -> dict:
    seeds = jax.random.split(jax.random.key(seed), 10)
    return {
        "queries": draw_queries(jax.random.fold_in(seeds[9], 71), 0),
        "key_proj": draw_key_proj(jax.random.fold_in(seeds[9], 71), 0),
        "value_proj": noise(seeds[2], (TOKENS, FEATS), 1.0, 6.0, ((0, 256),)),
        "residual": noise(seeds[3], (TOKENS, FEATS), 1.0, 6.0, ((0, 256),)),
        "query_gain": jnp.clip(jnp.exp(jax.random.uniform(seeds[4], (FEATS,), jnp.float32, math.log(1.0), math.log(3.0))), 1.0, 3.0),
        "key_gain": jnp.clip(jnp.exp(jax.random.uniform(seeds[5], (FEATS,), jnp.float32, math.log(1.0), math.log(3.0))), 1.0, 3.0),
        "gate_table": noise(seeds[6], (LEVELS, FEATS), 1.0, 6.0, (), jnp.float32),
        "noise_level": with_ends(jax.random.randint(seeds[7], (FRAMES,), 0, LEVELS), jax.random.fold_in(seeds[7], 1), 0, LEVELS - 1).astype(jnp.int32),
        "frame_reach": draw_frame_reach(jax.random.fold_in(seeds[9], 71), 0),
    }


def normalize(token_rows, gain_row):
    values = token_rows.astype(jnp.float32)
    square = lax.optimization_barrier(jnp.mean(values * values, axis=-1, keepdims=True))
    return (values * lax.rsqrt(square + 1e-06) * gain_row).astype(jnp.bfloat16)

def reference(queries, key_proj, value_proj, residual, query_gain, key_gain, gate_table, noise_level, frame_reach):
    query_norm = normalize(queries, query_gain)
    key_norm = normalize(key_proj, key_gain)
    score_scale = 1.0 / math.sqrt(HD)
    query_frame = jnp.arange(GROUP_TOK, dtype=jnp.int32) // FRAME_TOK
    key_frame = jnp.arange(2 * GROUP_TOK, dtype=jnp.int32) // FRAME_TOK - FRAMES_GRP

    def one_group(group_idx):
        start_row = (group_idx * GROUP_TOK).astype(jnp.int32)
        earlier = (jnp.maximum(group_idx - 1, 0) * GROUP_TOK).astype(jnp.int32)
        query_rows = lax.dynamic_slice_in_dim(query_norm, start_row, GROUP_TOK, 0).reshape(GROUP_TOK, HEADS, HD)
        keys_all = jnp.concatenate([lax.dynamic_slice_in_dim(key_norm, earlier, GROUP_TOK, 0), lax.dynamic_slice_in_dim(key_norm, start_row, GROUP_TOK, 0)], axis=0).reshape(2 * GROUP_TOK, HEADS, HD)
        values_all = jnp.concatenate([lax.dynamic_slice_in_dim(value_proj, earlier, GROUP_TOK, 0), lax.dynamic_slice_in_dim(value_proj, start_row, GROUP_TOK, 0)], axis=0).reshape(2 * GROUP_TOK, HEADS, HD)
        reach_here = lax.dynamic_slice_in_dim(frame_reach, (group_idx * FRAMES_GRP).astype(jnp.int32), FRAMES_GRP, 0)
        lower_frame = query_frame - reach_here[query_frame]
        key_live = (key_frame >= 0) | (group_idx > 0)
        allowed = (key_frame[None, :] >= lower_frame[:, None]) & key_live[None, :]

        def one_head(head_idx):
            query_head = lax.dynamic_index_in_dim(query_rows, head_idx, 1, keepdims=False)
            key_head = lax.dynamic_index_in_dim(keys_all, head_idx, 1, keepdims=False)
            value_head = lax.dynamic_index_in_dim(values_all, head_idx, 1, keepdims=False)
            scores = jnp.dot(query_head, key_head.T, preferred_element_type=jnp.float32) * score_scale
            scores = jnp.where(allowed, scores, -1e+30)
            highest = lax.optimization_barrier(jnp.max(scores, axis=-1, keepdims=True))
            exp_scores = jnp.exp(scores - highest)
            weights = (exp_scores / lax.optimization_barrier(jnp.sum(exp_scores, axis=-1, keepdims=True))).astype(jnp.bfloat16)
            return jnp.dot(weights, value_head, preferred_element_type=jnp.float32).astype(jnp.bfloat16)
        heads_out = lax.map(one_head, jnp.arange(HEADS, dtype=jnp.int32))
        return jnp.transpose(heads_out, (1, 0, 2)).reshape(GROUP_TOK, FEATS)
    attention = lax.map(one_group, jnp.arange(N_QUEUE, dtype=jnp.int32)).reshape(FRAMES, FRAME_TOK, FEATS)
    gate_rows = gate_table[noise_level]
    combined = residual.astype(jnp.float32).reshape(FRAMES, FRAME_TOK, FEATS) + gate_rows[:, None, :] * attention.astype(jnp.float32)
    advanced = combined.reshape(TOKENS, FEATS).astype(jnp.bfloat16)
    empty_rows = jnp.zeros((GROUP_TOK, FEATS), jnp.bfloat16)
    key_cache = jnp.concatenate([empty_rows, key_norm[:TOKENS - GROUP_TOK]], axis=0)
    value_cache = jnp.concatenate([empty_rows, value_proj[:TOKENS - GROUP_TOK]], axis=0)
    return (advanced, key_cache, value_cache)
```

```python
import math

import jax
import jax.numpy as jnp
from jax import lax
from jax.experimental import pallas as pl
from jax.experimental.pallas import tpu as pltpu
from jax.sharding import PartitionSpec as P

HD = 128
FRAMES_GRP = 4
FRAME_SLOTS = 4
PREP_ROWS = 32
LOG2E = 1.4426950408889634
SMEM = pltpu.SMEM
VMEM_LIMIT = 48 * 1024 * 1024


def normalize(token_rows, gain_row):
    values = token_rows.astype(jnp.float32)
    square = jnp.mean(values * values, axis=-1, keepdims=True)
    return (values * lax.rsqrt(square + 1e-06) * gain_row).astype(jnp.bfloat16)


def prep_kernel(q_ref, k_ref, v_ref, qg_ref, kg_ref, first_ref, second_ref, key_ref):
    rows, features = q_ref.shape
    query_norm = normalize(q_ref[...], qg_ref[...])
    key_norm = normalize(k_ref[...], kg_ref[...])
    key_ref[...] = key_norm
    for slot, whole in enumerate((v_ref[...], key_norm, query_norm)):
        for head in range(features // HD):
            target = second_ref if head % 2 else first_ref
            target[head // 2, slot] = whole[:, head * HD : (head + 1) * HD]


def prepare(queries, key_proj, value_proj, query_gain, key_gain):
    tok_dev, features = queries.shape
    slots = features // HD // 2
    row_block = pl.BlockSpec((PREP_ROWS, features), lambda i: (i, 0))
    gain_block = pl.BlockSpec((1, features), lambda i: (0, 0))
    item_block = pl.BlockSpec((slots, 3, PREP_ROWS, HD), lambda i: (0, 0, i, 0))
    items = jax.ShapeDtypeStruct((slots, 3, tok_dev, HD), jnp.bfloat16)
    return pl.pallas_call(
        prep_kernel,
        grid=(tok_dev // PREP_ROWS,),
        in_specs=[row_block, row_block, row_block, gain_block, gain_block],
        out_specs=[item_block, item_block, row_block],
        out_shape=[items, items, jax.ShapeDtypeStruct((tok_dev, features), jnp.bfloat16)],
        compiler_params=pltpu.CompilerParams(vmem_limit_bytes=VMEM_LIMIT),
        cost_estimate=pl.CostEstimate(flops=8_000_000, bytes_accessed=8_000_000, transcendentals=0),
        name="prep",
    )(queries, key_proj, value_proj, query_gain.reshape(1, -1), key_gain.reshape(1, -1))


def attend_kernel(place_ref, reach_ref, own_ref, prior_ref, out_ref):
    frame = pl.program_id(0)
    queue_pos = place_ref[0]
    lowest = jnp.where(queue_pos > 0, -FRAMES_GRP, 0)
    lower = jnp.maximum(frame - reach_ref[queue_pos * FRAMES_GRP + frame], lowest)
    rows = FRAME_SLOTS * own_ref.shape[2]
    query = own_ref[pl.ds(frame * FRAME_SLOTS, FRAME_SLOTS), 2].reshape(rows, HD)
    scale = LOG2E / math.sqrt(HD)

    def tile(key, value, carry):
        highest, total, mixed = carry
        scores = lax.dot_general(
            key, query, (((1,), (1,)), ((), ())), preferred_element_type=jnp.float32
        )
        raised = jnp.maximum(highest, jnp.max(scores, axis=0, keepdims=True))
        fade = jnp.exp2((highest - raised) * scale)
        weights = jnp.exp2((scores - raised) * scale)
        total = total * fade + jnp.sum(weights, axis=0, keepdims=True)
        part = lax.dot_general(
            value,
            weights.astype(jnp.bfloat16),
            (((0,), (0,)), ((), ())),
            preferred_element_type=jnp.float32,
        )
        return raised, total, mixed * fade + part

    def own_tile(step, carry):
        at = pl.ds(step * FRAME_SLOTS, FRAME_SLOTS)
        return tile(own_ref[at, 1].reshape(rows, HD), own_ref[at, 0].reshape(rows, HD), carry)

    def prior_tile(step, carry):
        at = pl.ds((step + FRAMES_GRP) * FRAME_SLOTS, FRAME_SLOTS)
        return tile(prior_ref[at, 1].reshape(rows, HD), prior_ref[at, 0].reshape(rows, HD), carry)

    carry = (
        jnp.full((1, rows), -1e30, jnp.float32),
        jnp.zeros((1, rows), jnp.float32),
        jnp.zeros((HD, rows), jnp.float32),
    )
    carry = lax.fori_loop(jnp.maximum(lower, 0), FRAMES_GRP, own_tile, carry)
    carry = lax.fori_loop(jnp.minimum(lower, 0), 0, prior_tile, carry)
    _, total, mixed = carry
    result = (mixed / total).T.astype(jnp.bfloat16)
    out_ref[...] = result.reshape(out_ref.shape)


def attend(place, frame_reach, own, prior):
    slots, _, tok_dev, _ = own.shape
    return pl.pallas_call(
        attend_kernel,
        grid=(FRAMES_GRP,),
        in_specs=[
            pl.BlockSpec(memory_space=SMEM),
            pl.BlockSpec(memory_space=SMEM),
            pl.BlockSpec(own.shape, lambda i: (0, 0, 0, 0)),
            pl.BlockSpec(prior.shape, lambda i: (0, 0, 0, 0)),
        ],
        out_specs=pl.BlockSpec((FRAME_SLOTS, tok_dev, HD), lambda i: (i, 0, 0)),
        out_shape=jax.ShapeDtypeStruct((slots, tok_dev, HD), jnp.bfloat16),
        compiler_params=pltpu.CompilerParams(vmem_limit_bytes=VMEM_LIMIT),
        cost_estimate=pl.CostEstimate(
            flops=4_000_000_000, bytes_accessed=3_000_000, transcendentals=8_000_000
        ),
        name="attend",
    )(place, frame_reach, own, prior)


def finish_kernel(place_ref, level_ref, first_ref, second_ref, residual_ref, gate_ref, out_ref):
    level = level_ref[place_ref[0] * FRAMES_GRP + place_ref[1] // FRAME_SLOTS]
    gate = gate_ref[pl.ds(level, 1), :]
    for head in range(residual_ref.shape[1] // HD):
        source = second_ref if head % 2 else first_ref
        at = slice(head * HD, (head + 1) * HD)
        mixed = gate[:, at] * source[head // 2].astype(jnp.float32)
        out_ref[:, at] = (residual_ref[:, at].astype(jnp.float32) + mixed).astype(jnp.bfloat16)


def finish(place, noise_level, first, second, residual, gate_table):
    tok_dev, features = residual.shape
    blocks = 4
    wide = features // blocks
    slots = first.shape[0] // blocks
    item_block = pl.BlockSpec((slots, tok_dev, HD), lambda i: (i, 0, 0))
    row_block = pl.BlockSpec((tok_dev, wide), lambda i: (0, i))
    return pl.pallas_call(
        finish_kernel,
        grid=(blocks,),
        in_specs=[
            pl.BlockSpec(memory_space=SMEM),
            pl.BlockSpec(memory_space=SMEM),
            item_block,
            item_block,
            row_block,
            pl.BlockSpec((gate_table.shape[0], wide), lambda i: (0, i)),
        ],
        out_specs=row_block,
        out_shape=jax.ShapeDtypeStruct(residual.shape, jnp.bfloat16),
        compiler_params=pltpu.CompilerParams(vmem_limit_bytes=VMEM_LIMIT),
        name="finish",
    )(place, noise_level, first, second, residual, gate_table)


def shifted(shard):
    devices = lax.axis_size("queue")
    return lax.ppermute(shard, "queue", [(i, i + 1) for i in range(devices - 1)])


def exchange(items):
    return lax.all_to_all(items, "head", split_axis=0, concat_axis=0, tiled=True)


def shards(
    queries,
    key_proj,
    value_proj,
    residual,
    query_gain,
    key_gain,
    gate_table,
    noise_level,
    frame_reach,
):
    place = jnp.stack([lax.axis_index("queue"), lax.axis_index("head")]).astype(jnp.int32)
    first, second, key_norm = prepare(queries, key_proj, value_proj, query_gain, key_gain)
    own_first = exchange(first)
    prior_first = shifted(own_first[:, :2])
    own_second = exchange(second)
    prior_second = shifted(own_second[:, :2])
    value_cache = shifted(value_proj)
    key_cache = shifted(key_norm)
    out_first = exchange(attend(place, frame_reach, own_first, prior_first))
    out_second = exchange(attend(place, frame_reach, own_second, prior_second))
    advanced = finish(place, noise_level, out_first, out_second, residual, gate_table)
    return (advanced, key_cache, value_cache)


def solution(mesh):
    return jax.shard_map(
        shards,
        mesh=mesh,
        in_specs=(
            P(("queue", "head"), None),
            P(("queue", "head"), None),
            P(("queue", "head"), None),
            P(("queue", "head"), None),
            P(),
            P(),
            P(),
            P(),
            P(),
        ),
        out_specs=(
            P(("queue", "head"), None),
            P(("queue", "head"), None),
            P(("queue", "head"), None),
        ),
        check_vma=False,
    )
```

```python
import math

import jax
import jax.numpy as jnp
from jax import lax
from jax.experimental import pallas as pl
from jax.experimental.pallas import tpu as pltpu
from jax.sharding import PartitionSpec as P

HD = 128
FRAMES_GRP = 4
FRAME_SLOTS = 4
PREP_ROWS = 32
QUERY_ROWS = 256
WRAP_TO = 8
RELAYS = (None, 0, 3, 5)
LOG2E = 1.4426950408889634
SMEM = pltpu.SMEM
VMEM_LIMIT = 60 * 1024 * 1024


def normalize(token_rows, gain_row):
    values = token_rows.astype(jnp.float32)
    square = jnp.mean(values * values, axis=-1, keepdims=True)
    return (values * lax.rsqrt(square + 1e-06) * gain_row).astype(jnp.bfloat16)


def prep_keys_kernel(k_ref, v_ref, gain_ref, items_ref, key_ref):
    value = v_ref[...]
    key_norm = normalize(k_ref[...], gain_ref[...])
    key_ref[...] = key_norm
    for head in range(k_ref.shape[1] // HD):
        at = slice(head * HD, (head + 1) * HD)
        items_ref[head // 2, 2 * (head % 2)] = value[:, at]
        items_ref[head // 2, 2 * (head % 2) + 1] = key_norm[:, at]


def prep_keys(key_proj, value_proj, key_gain):
    tok_dev, features = key_proj.shape
    slots = features // HD // 2
    row_block = pl.BlockSpec((PREP_ROWS, features), lambda i: (i, 0))
    return pl.pallas_call(
        prep_keys_kernel,
        grid=(tok_dev // PREP_ROWS,),
        in_specs=[row_block, row_block, pl.BlockSpec((1, features), lambda i: (0, 0))],
        out_specs=[pl.BlockSpec((slots, 4, PREP_ROWS, HD), lambda i: (0, 0, i, 0)), row_block],
        out_shape=[
            jax.ShapeDtypeStruct((slots, 4, tok_dev, HD), jnp.bfloat16),
            jax.ShapeDtypeStruct((tok_dev, features), jnp.bfloat16),
        ],
        compiler_params=pltpu.CompilerParams(vmem_limit_bytes=VMEM_LIMIT),
        cost_estimate=pl.CostEstimate(flops=4_000_000, bytes_accessed=5_000_000, transcendentals=0),
        name="prep_keys",
    )(key_proj, value_proj, key_gain.reshape(1, -1))


def prep_queries_kernel(q_ref, gain_ref, items_ref):
    query_norm = normalize(q_ref[...], gain_ref[...])
    for head in range(q_ref.shape[1] // HD):
        items_ref[head // 2, head % 2] = query_norm[:, head * HD : (head + 1) * HD]


def prep_queries(queries, query_gain):
    tok_dev, features = queries.shape
    slots = features // HD // 2
    return pl.pallas_call(
        prep_queries_kernel,
        grid=(tok_dev // PREP_ROWS,),
        in_specs=[
            pl.BlockSpec((PREP_ROWS, features), lambda i: (i, 0)),
            pl.BlockSpec((1, features), lambda i: (0, 0)),
        ],
        out_specs=pl.BlockSpec((slots, 2, PREP_ROWS, HD), lambda i: (0, 0, i, 0)),
        out_shape=jax.ShapeDtypeStruct((slots, 2, tok_dev, HD), jnp.bfloat16),
        compiler_params=pltpu.CompilerParams(vmem_limit_bytes=VMEM_LIMIT),
        cost_estimate=pl.CostEstimate(flops=4_000_000, bytes_accessed=3_000_000, transcendentals=0),
        name="prep_queries",
    )(queries, query_gain.reshape(1, -1))


def attend_kernel(
    place_ref,
    reach_ref,
    query_ref,
    own_value,
    own_key,
    main_ref,
    *refs,
):
    *far_refs, out_ref, mixed_ref, lanes_ref, held_ref, sems = refs
    head, frame = pl.program_id(0), pl.program_id(1)
    queue_pos = place_ref[0]
    lowest = jnp.where(queue_pos > 0, -FRAMES_GRP, 0)
    lower = jnp.maximum(frame - reach_ref[queue_pos * FRAMES_GRP + frame], lowest)
    own_from = jnp.maximum(lower, 0)
    prior_from = jnp.minimum(lower, 0) + FRAMES_GRP
    far = queue_pos == WRAP_TO
    share = held_ref.shape[0] // len(far_refs)

    def loads(source_of):
        for part in range(len(far_refs)):
            at = pl.ds(part * share, share)
            yield pltpu.make_async_copy(source_of(part, at), held_ref.at[at], sems.at[part])

    @pl.when((head == 0) & (frame == 0) & far)
    def _():
        for load in loads(lambda part, at: far_refs[part]):
            load.start()

    @pl.when((head == 0) & (frame == 0) & jnp.logical_not(far))
    def _():
        for load in loads(lambda part, at: main_ref.at[at]):
            load.start()

    prior_value = held_ref.at[:, 2 * head]
    prior_key = held_ref.at[:, 2 * head + 1]
    rows = query_ref.shape[0] * query_ref.shape[1]
    scale = LOG2E / math.sqrt(HD)

    def scores_of(query, key):
        return lax.dot_general(
            query, key, (((1,), (1,)), ((), ())), preferred_element_type=jnp.float32
        )

    def block(ref, start, count):
        slots = ref[pl.ds(start * FRAME_SLOTS, count * FRAME_SLOTS)]
        return slots.reshape(count * rows, HD)

    def plain(key_ref, value_ref, start, add):
        key = block(key_ref, start, FRAMES_GRP - start)
        value = block(value_ref, start, FRAMES_GRP - start)
        query = query_ref[...].reshape(rows, HD)
        for low in range(0, rows, QUERY_ROWS):
            at = slice(low, low + QUERY_ROWS)
            weights = jnp.exp2(scores_of(query[at], key) * scale)
            lanes = lanes_ref[at] if add else 0.0
            for col in range(0, weights.shape[1], HD):
                lanes = lanes + weights[:, col : col + HD]
            mixed = jnp.dot(
                weights.astype(jnp.bfloat16), value, preferred_element_type=jnp.float32
            )
            lanes_ref[at] = lanes
            mixed_ref[at] = mixed_ref[at] + mixed if add else mixed

    for start in range(FRAMES_GRP):

        @pl.when(own_from == start)
        def _(start=start):
            plain(own_key, own_value, start, False)

    @pl.when((head == 0) & (frame == 0))
    def _():
        for load in loads(lambda part, at: main_ref.at[at]):
            load.wait()

    for start in range(FRAMES_GRP):

        @pl.when(prior_from == start)
        def _(start=start):
            plain(prior_key, prior_value, start, True)

    def store(mixed, total):
        out_ref[...] = (mixed / total).astype(jnp.bfloat16).reshape(out_ref.shape)

    total = jnp.sum(lanes_ref[...], axis=1, keepdims=True)
    store(mixed_ref[...], total)
    inside = (jnp.max(total) < 1e37) & (jnp.min(total) > 1e-25)

    @pl.when(jnp.logical_not(inside))
    def _():
        query = query_ref[...].reshape(rows, HD)

        def tile(key, value, carry):
            highest, total, mixed = carry
            scores = scores_of(query, key)
            raised = jnp.maximum(highest, jnp.max(scores, axis=1, keepdims=True))
            fade = jnp.exp2((highest - raised) * scale)
            weights = jnp.exp2((scores - raised) * scale)
            total = total * fade + jnp.sum(weights, axis=1, keepdims=True)
            part = jnp.dot(weights.astype(jnp.bfloat16), value, preferred_element_type=jnp.float32)
            return raised, total, mixed * fade + part

        def own_tile(step, carry):
            return tile(block(own_key, step, 1), block(own_value, step, 1), carry)

        def prior_tile(step, carry):
            return tile(block(prior_key, step, 1), block(prior_value, step, 1), carry)

        start = jnp.full((rows, 1), -1e30, jnp.float32)
        carry = (start, jnp.zeros_like(start), jnp.zeros((rows, HD), jnp.float32))
        carry = lax.fori_loop(own_from, FRAMES_GRP, own_tile, carry)
        _, total, mixed = lax.fori_loop(prior_from, FRAMES_GRP, prior_tile, carry)
        store(mixed, total)


def attend(place, frame_reach, query, own, main, far):
    slots, heads, tok_dev, _ = query.shape
    rows = FRAME_SLOTS * tok_dev
    frame_block = pl.BlockSpec((FRAME_SLOTS, None, tok_dev, HD), lambda h, i: (i, h, 0, 0))
    value_block = pl.BlockSpec((slots, None, tok_dev, HD), lambda h, i: (0, 2 * h, 0, 0))
    key_block = pl.BlockSpec((slots, None, tok_dev, HD), lambda h, i: (0, 2 * h + 1, 0, 0))
    return pl.pallas_call(
        attend_kernel,
        grid=(heads, FRAMES_GRP),
        in_specs=[
            pl.BlockSpec(memory_space=SMEM),
            pl.BlockSpec(memory_space=SMEM),
            frame_block,
            value_block,
            key_block,
            *[pl.BlockSpec(memory_space=pl.ANY) for _ in (main, *far)],
        ],
        out_specs=frame_block,
        out_shape=jax.ShapeDtypeStruct(query.shape, jnp.bfloat16),
        scratch_shapes=[
            pltpu.VMEM((rows, HD), jnp.float32),
            pltpu.VMEM((rows, HD), jnp.float32),
            pltpu.VMEM(main.shape, jnp.bfloat16),
            pltpu.SemaphoreType.DMA((len(far),)),
        ],
        compiler_params=pltpu.CompilerParams(vmem_limit_bytes=VMEM_LIMIT),
        cost_estimate=pl.CostEstimate(
            flops=16_000_000_000, bytes_accessed=6_000_000, transcendentals=16_000_000
        ),
        name="attend",
    )(place, frame_reach, query, own, own, main, *far)


def finish_kernel(
    place_ref,
    gate_ref,
    mixed_ref,
    residual_ref,
    key_main,
    key_late,
    value_main,
    value_late,
    out_ref,
    key_out,
    value_out,
    key_held,
    value_held,
    sems,
):
    step = pl.program_id(0)
    late = (place_ref[0] == WRAP_TO) | (place_ref[0] == 0)
    keys_in = pltpu.make_async_copy(key_main, key_held, sems.at[0])
    late_keys_in = pltpu.make_async_copy(key_late, key_held, sems.at[0])
    values_in = pltpu.make_async_copy(value_main, value_held, sems.at[1])
    late_values_in = pltpu.make_async_copy(value_late, value_held, sems.at[1])
    keys_out = pltpu.make_async_copy(key_held, key_out, sems.at[2])
    values_out = pltpu.make_async_copy(value_held, value_out, sems.at[3])

    @pl.when(step == 0)
    def _():
        @pl.when(late)
        def _():
            late_keys_in.start()
            late_values_in.start()

        @pl.when(jnp.logical_not(late))
        def _():
            keys_in.start()
            values_in.start()

    for head in range(residual_ref.shape[1] // HD):
        at = slice(head * HD, (head + 1) * HD)
        mixed = gate_ref[:, at] * mixed_ref[head // 2, head % 2].astype(jnp.float32)
        out_ref[:, at] = (residual_ref[:, at].astype(jnp.float32) + mixed).astype(jnp.bfloat16)

    @pl.when(step == 1)
    def _():
        keys_in.wait()
        keys_out.start()
        values_in.wait()
        values_out.start()

    @pl.when(step == pl.num_programs(0) - 1)
    def _():
        keys_out.wait()
        values_out.wait()


def finish(place, gate_row, mixed, residual, key_main, key_late, value_main, value_late):
    tok_dev, features = residual.shape
    blocks = 4
    wide = features // blocks
    row_block = pl.BlockSpec((tok_dev, wide), lambda i: (0, i))
    item_block = pl.BlockSpec((mixed.shape[0] // blocks, 2, tok_dev, HD), lambda i: (i, 0, 0, 0))
    anywhere = pl.BlockSpec(memory_space=pl.ANY)
    whole = jax.ShapeDtypeStruct(residual.shape, jnp.bfloat16)
    return pl.pallas_call(
        finish_kernel,
        grid=(blocks,),
        in_specs=[
            pl.BlockSpec(memory_space=SMEM),
            pl.BlockSpec((1, wide), lambda i: (0, i)),
            item_block,
            row_block,
            anywhere,
            anywhere,
            anywhere,
            anywhere,
        ],
        out_specs=[row_block, anywhere, anywhere],
        out_shape=[whole, whole, whole],
        scratch_shapes=[
            pltpu.VMEM(residual.shape, jnp.bfloat16),
            pltpu.VMEM(residual.shape, jnp.bfloat16),
            pltpu.SemaphoreType.DMA((4,)),
        ],
        compiler_params=pltpu.CompilerParams(vmem_limit_bytes=VMEM_LIMIT),
        name="finish",
    )(place, gate_row, mixed, residual, key_main, key_late, value_main, value_late)


def moved(shard, *pairs):
    return lax.ppermute(shard, "queue", list(pairs))


def inner_pairs():
    return [(i, i + 1) for i in range(lax.axis_size("queue") - 1) if i + 1 != WRAP_TO]


def far_parts(own):
    share = own.shape[0] // len(RELAYS)
    parts = []
    for index, relay in enumerate(RELAYS):
        part = own[index * share : (index + 1) * share]
        if relay is None:
            parts.append(moved(part, (WRAP_TO - 1, WRAP_TO)))
        else:
            parts.append(moved(moved(part, (WRAP_TO - 1, relay)), (relay, WRAP_TO)))
    return parts


def exchange(items):
    return lax.all_to_all(items, "head", split_axis=0, concat_axis=0, tiled=True)


def shards(
    queries,
    key_proj,
    value_proj,
    residual,
    query_gain,
    key_gain,
    gate_table,
    noise_level,
    frame_reach,
):
    queue_pos, head_pos = lax.axis_index("queue"), lax.axis_index("head")
    place = jnp.stack([queue_pos, head_pos]).astype(jnp.int32)
    frame = queue_pos * FRAMES_GRP + head_pos // FRAME_SLOTS
    level = lax.dynamic_index_in_dim(noise_level, frame, 0, keepdims=False)
    gate_row = lax.dynamic_slice_in_dim(gate_table, level, 1, 0)
    items, key_norm = prep_keys(key_proj, value_proj, key_gain)
    value_main = moved(value_proj, *inner_pairs(), (WRAP_TO - 1, 0))
    key_main = moved(key_norm, *inner_pairs())
    own = exchange(items)
    query_items = prep_queries(queries, query_gain)
    own, query_items, value_main, key_main, gate_row, place = lax.optimization_barrier(
        (own, query_items, value_main, key_main, gate_row, place)
    )
    main = moved(own, *inner_pairs())
    far = far_parts(own)
    query_items = exchange(query_items)
    query_items, main, far, key_norm, value_main = lax.optimization_barrier(
        (query_items, main, far, key_norm, value_main)
    )
    key_late = moved(key_norm, (WRAP_TO - 1, WRAP_TO))
    value_late = moved(value_main, (0, WRAP_TO))
    mixed = attend(place, frame_reach, query_items, own, main, far)
    mixed, key_late, value_late = lax.optimization_barrier((mixed, key_late, value_late))
    mixed = exchange(mixed)
    advanced, key_cache, value_cache = finish(
        place, gate_row, mixed, residual, key_main, key_late, value_main, value_late
    )
    return (advanced, key_cache, value_cache)


def solution(mesh):
    return jax.shard_map(
        shards,
        mesh=mesh,
        in_specs=(
            P(("queue", "head"), None),
            P(("queue", "head"), None),
            P(("queue", "head"), None),
            P(("queue", "head"), None),
            P(),
            P(),
            P(),
            P(),
            P(),
        ),
        out_specs=(
            P(("queue", "head"), None),
            P(("queue", "head"), None),
            P(("queue", "head"), None),
        ),
        check_vma=False,
    )
```

```python
import math

import jax
import jax.numpy as jnp
from jax import lax
from jax.experimental import pallas as pl
from jax.experimental.pallas import tpu as pltpu
from jax.sharding import PartitionSpec as P

HD = 128
FRAMES_GRP = 4
FRAME_SLOTS = 4
PREP_ROWS = 64
CACHE_PARTS = 4
QUERY_ROWS = 256
WRAP_TO = 8
KEY_RELAY, VALUE_RELAY = 3, 0
LOG2E = 1.4426950408889634
SMEM = pltpu.SMEM
VMEM_LIMIT = 60 * 1024 * 1024


def normalize(token_rows, gain_row):
    values = token_rows.astype(jnp.float32)
    square = jnp.mean(values * values, axis=-1, keepdims=True)
    return (values * lax.rsqrt(square + 1e-06) * gain_row).astype(jnp.bfloat16)


def prep_kernel(q_ref, k_ref, v_ref, qg_ref, kg_ref, early_ref, late_ref, key_ref):
    value = v_ref[...]
    key_norm = normalize(k_ref[...], kg_ref[...])
    query_norm = normalize(q_ref[...], qg_ref[...])
    key_ref[...] = key_norm
    for head in range(q_ref.shape[1] // HD):
        at = slice(head * HD, (head + 1) * HD)
        slot, second = head // 2, head % 2
        early_ref[slot, 2 * second] = value[:, at]
        early_ref[slot, 2 * second + 1] = key_norm[:, at]
        if second:
            late_ref[slot, 0] = query_norm[:, at]
        else:
            early_ref[slot, 4] = query_norm[:, at]


def prepare(queries, key_proj, value_proj, query_gain, key_gain):
    tok_dev, features = queries.shape
    slots = features // HD // 2
    row_block = pl.BlockSpec((PREP_ROWS, features), lambda i: (i, 0))
    gain_block = pl.BlockSpec((1, features), lambda i: (0, 0))
    return pl.pallas_call(
        prep_kernel,
        grid=(tok_dev // PREP_ROWS,),
        in_specs=[row_block, row_block, row_block, gain_block, gain_block],
        out_specs=[
            pl.BlockSpec((slots, 5, PREP_ROWS, HD), lambda i: (0, 0, i, 0)),
            pl.BlockSpec((slots, 1, PREP_ROWS, HD), lambda i: (0, 0, i, 0)),
            row_block,
        ],
        out_shape=[
            jax.ShapeDtypeStruct((slots, 5, tok_dev, HD), jnp.bfloat16),
            jax.ShapeDtypeStruct((slots, 1, tok_dev, HD), jnp.bfloat16),
            jax.ShapeDtypeStruct((tok_dev, features), jnp.bfloat16),
        ],
        compiler_params=pltpu.CompilerParams(vmem_limit_bytes=VMEM_LIMIT),
        cost_estimate=pl.CostEstimate(flops=8_000_000, bytes_accessed=8_000_000, transcendentals=0),
        name="prep",
    )(queries, key_proj, value_proj, query_gain.reshape(1, -1), key_gain.reshape(1, -1))


def attend_kernel(
    place_ref,
    reach_ref,
    query_ref,
    own_value,
    own_key,
    *refs,
):
    *priors, out_ref, total_ref, held_ref, sems = refs
    frame = pl.program_id(0)
    queue_pos = place_ref[0]
    main, *far = priors

    @pl.when((frame == 0) & ((queue_pos != WRAP_TO) | (not far)))
    def _():
        load = pltpu.make_async_copy(main, held_ref, sems.at[0])
        load.start()
        load.wait()

    if far:

        @pl.when((frame == 0) & (queue_pos == WRAP_TO))
        def _():
            loads = [
                pltpu.make_async_copy(part, held_ref.at[:, at], sems.at[at])
                for at, part in enumerate(far)
            ]
            for load in loads:
                load.start()
            for load in loads:
                load.wait()

    prior_value, prior_key = held_ref.at[:, 0], held_ref.at[:, 1]
    lowest = jnp.where(queue_pos > 0, -FRAMES_GRP, 0)
    lower = jnp.maximum(frame - reach_ref[queue_pos * FRAMES_GRP + frame], lowest)
    own_from = jnp.maximum(lower, 0)
    prior_from = jnp.minimum(lower, 0) + FRAMES_GRP
    rows = query_ref.shape[0] * query_ref.shape[1]
    scale = LOG2E / math.sqrt(HD)

    def scores_of(query, key):
        return lax.dot_general(
            query, key, (((1,), (1,)), ((), ())), preferred_element_type=jnp.float32
        )

    def block(ref, start, count):
        slots = ref[pl.ds(start * FRAME_SLOTS, count * FRAME_SLOTS)]
        return slots.reshape(count * rows, HD)

    def plain(parts):
        pairs = [
            (block(key_ref, start, FRAMES_GRP - start), block(value_ref, start, FRAMES_GRP - start))
            for key_ref, value_ref, start in parts
        ]
        query = query_ref[...].reshape(rows, HD)
        for low in range(0, rows, QUERY_ROWS):
            at = slice(low, low + QUERY_ROWS)
            lanes, mixed = None, None
            for key, value in pairs:
                weights = jnp.exp2(scores_of(query[at], key) * scale)
                part = jnp.dot(
                    weights.astype(jnp.bfloat16), value, preferred_element_type=jnp.float32
                )
                mixed = part if mixed is None else mixed + part
                for col in range(0, weights.shape[1], HD):
                    one = weights[:, col : col + HD]
                    lanes = one if lanes is None else lanes + one
            total = jnp.sum(lanes, axis=1, keepdims=True)
            slot = low // out_ref.shape[1]
            count = QUERY_ROWS // out_ref.shape[1]
            result = (mixed / total).astype(jnp.bfloat16)
            out_ref[slot : slot + count] = result.reshape(count, *out_ref.shape[1:])
            total_ref[at] = total

    for start in range(FRAMES_GRP):

        @pl.when((own_from == start) & (prior_from == FRAMES_GRP))
        def _(start=start):
            plain([(own_key, own_value, start)])

        @pl.when(prior_from == start)
        def _(start=start):
            plain([(own_key, own_value, 0), (prior_key, prior_value, start)])

    def store(mixed, total):
        out_ref[...] = (mixed / total).astype(jnp.bfloat16).reshape(out_ref.shape)

    total = total_ref[...]
    inside = (jnp.max(total) < 1e37) & (jnp.min(total) > 1e-25)

    @pl.when(jnp.logical_not(inside))
    def _():
        query = query_ref[...].reshape(rows, HD)

        def tile(key, value, carry):
            highest, total, mixed = carry
            scores = scores_of(query, key)
            raised = jnp.maximum(highest, jnp.max(scores, axis=1, keepdims=True))
            fade = jnp.exp2((highest - raised) * scale)
            weights = jnp.exp2((scores - raised) * scale)
            total = total * fade + jnp.sum(weights, axis=1, keepdims=True)
            part = jnp.dot(weights.astype(jnp.bfloat16), value, preferred_element_type=jnp.float32)
            return raised, total, mixed * fade + part

        def own_tile(step, carry):
            return tile(block(own_key, step, 1), block(own_value, step, 1), carry)

        def prior_tile(step, carry):
            return tile(block(prior_key, step, 1), block(prior_value, step, 1), carry)

        start = jnp.full((rows, 1), -1e30, jnp.float32)
        carry = (start, jnp.zeros_like(start), jnp.zeros((rows, HD), jnp.float32))
        carry = lax.fori_loop(own_from, FRAMES_GRP, own_tile, carry)
        _, total, mixed = lax.fori_loop(prior_from, FRAMES_GRP, prior_tile, carry)
        store(mixed, total)


def attend(place, frame_reach, query, own, *priors):
    query, query_at = query
    own, own_at = own
    slots, _, tok_dev, _ = own.shape
    rows = FRAME_SLOTS * tok_dev

    def whole(index):
        return pl.BlockSpec((slots, None, tok_dev, HD), lambda i: (0, index, 0, 0))

    return pl.pallas_call(
        attend_kernel,
        grid=(FRAMES_GRP,),
        in_specs=[
            pl.BlockSpec(memory_space=SMEM),
            pl.BlockSpec(memory_space=SMEM),
            pl.BlockSpec((FRAME_SLOTS, None, tok_dev, HD), lambda i: (i, query_at, 0, 0)),
            whole(own_at),
            whole(own_at + 1),
            *[pl.BlockSpec(memory_space=pl.ANY) for _ in priors],
        ],
        out_specs=pl.BlockSpec((FRAME_SLOTS, tok_dev, HD), lambda i: (i, 0, 0)),
        out_shape=jax.ShapeDtypeStruct((slots, tok_dev, HD), jnp.bfloat16),
        scratch_shapes=[
            pltpu.VMEM((rows, 1), jnp.float32),
            pltpu.VMEM(priors[0].shape, jnp.bfloat16),
            pltpu.SemaphoreType.DMA((2,)),
        ],
        compiler_params=pltpu.CompilerParams(vmem_limit_bytes=VMEM_LIMIT),
        cost_estimate=pl.CostEstimate(
            flops=8_000_000_000, bytes_accessed=3_000_000, transcendentals=8_000_000
        ),
        name="attend",
    )(place, frame_reach, query, own, own, *priors)


def place_kernel(
    place_ref,
    key_main,
    key_late,
    value_main,
    value_late,
    key_out,
    value_out,
    key_held,
    value_held,
    sems,
):
    late = place_ref[0] == WRAP_TO
    rows = key_held.shape[0] // CACHE_PARTS
    for part in range(CACHE_PARTS):
        at = pl.ds(part * rows, rows)

        def load(source, held, index, at=at, part=part):
            return pltpu.make_async_copy(source.at[at], held.at[at], sems.at[index, part])

        @pl.when(late)
        def _(load=load):
            load(key_late, key_held, 0).start()
            load(value_late, value_held, 1).start()

        @pl.when(jnp.logical_not(late))
        def _(load=load):
            load(key_main, key_held, 0).start()
            load(value_main, value_held, 1).start()

    stores = []
    for part in range(CACHE_PARTS):
        at = pl.ds(part * rows, rows)
        for index, source, held, out in (
            (0, key_main, key_held, key_out),
            (1, value_main, value_held, value_out),
        ):
            pltpu.make_async_copy(source.at[at], held.at[at], sems.at[index, part]).wait()
            store = pltpu.make_async_copy(held.at[at], out.at[at], sems.at[index + 2, part])
            store.start()
            stores.append(store)
    for store in stores:
        store.wait()


def place_caches(place, key_main, key_late, value_main, value_late):
    anywhere = pl.BlockSpec(memory_space=pl.ANY)
    whole = jax.ShapeDtypeStruct(key_main.shape, jnp.bfloat16)
    return pl.pallas_call(
        place_kernel,
        in_specs=[pl.BlockSpec(memory_space=SMEM), anywhere, anywhere, anywhere, anywhere],
        out_specs=[anywhere, anywhere],
        out_shape=[whole, whole],
        scratch_shapes=[
            pltpu.VMEM(key_main.shape, jnp.bfloat16),
            pltpu.VMEM(key_main.shape, jnp.bfloat16),
            pltpu.SemaphoreType.DMA((4, CACHE_PARTS)),
        ],
        compiler_params=pltpu.CompilerParams(vmem_limit_bytes=VMEM_LIMIT),
        cost_estimate=pl.CostEstimate(flops=0, bytes_accessed=4_000_000, transcendentals=0),
        name="place_caches",
    )(place, key_main, key_late, value_main, value_late)


def finish_kernel(gate_ref, first_ref, second_ref, residual_ref, out_ref):
    for head in range(residual_ref.shape[1] // HD):
        source = second_ref if head % 2 else first_ref
        at = slice(head * HD, (head + 1) * HD)
        mixed = gate_ref[:, at] * source[head // 2].astype(jnp.float32)
        out_ref[:, at] = (residual_ref[:, at].astype(jnp.float32) + mixed).astype(jnp.bfloat16)


def finish(gate_row, first, second, residual):
    tok_dev, features = residual.shape
    blocks = 2
    wide = features // blocks
    row_block = pl.BlockSpec((tok_dev, wide), lambda i: (0, i))
    item_block = pl.BlockSpec((first.shape[0] // blocks, tok_dev, HD), lambda i: (i, 0, 0))
    return pl.pallas_call(
        finish_kernel,
        grid=(blocks,),
        in_specs=[
            pl.BlockSpec((1, wide), lambda i: (0, i)),
            item_block,
            item_block,
            row_block,
        ],
        out_specs=row_block,
        out_shape=jax.ShapeDtypeStruct(residual.shape, jnp.bfloat16),
        compiler_params=pltpu.CompilerParams(vmem_limit_bytes=VMEM_LIMIT),
        name="finish",
    )(gate_row, first, second, residual)


def moved(shard, *pairs):
    return lax.ppermute(shard, "queue", list(pairs))


def inner_pairs():
    return [(i, i + 1) for i in range(lax.axis_size("queue") - 1) if i + 1 != WRAP_TO]


def exchange(items):
    return lax.all_to_all(items, "head", split_axis=0, concat_axis=0, tiled=True)


def shards(
    queries,
    key_proj,
    value_proj,
    residual,
    query_gain,
    key_gain,
    gate_table,
    noise_level,
    frame_reach,
):
    queue_pos, head_pos = lax.axis_index("queue"), lax.axis_index("head")
    place = jnp.stack([queue_pos, head_pos]).astype(jnp.int32)
    frame = queue_pos * FRAMES_GRP + head_pos // FRAME_SLOTS
    level = lax.dynamic_index_in_dim(noise_level, frame, 0, keepdims=False)
    gate_row = lax.dynamic_slice_in_dim(gate_table, level, 1, 0)
    early, late, key_norm = prepare(queries, key_proj, value_proj, query_gain, key_gain)
    inner = inner_pairs()
    every = (*inner, (WRAP_TO - 1, WRAP_TO))
    value_main = moved(value_proj, *inner)
    key_main = moved(key_norm, *inner)
    value_half = moved(value_proj, (WRAP_TO - 1, VALUE_RELAY))
    key_half = moved(key_norm, (WRAP_TO - 1, KEY_RELAY))
    early = exchange(early)
    early, late, value_main, key_main, value_half, key_half, gate_row, place = (
        lax.optimization_barrier(
            (early, late, value_main, key_main, value_half, key_half, gate_row, place)
        )
    )
    key_late = moved(key_half, (KEY_RELAY, WRAP_TO))
    value_late = moved(value_half, (VALUE_RELAY, WRAP_TO))
    wrap = (WRAP_TO - 1, WRAP_TO)
    prior_first = moved(early[:, 0:2], *every)
    prior_second = moved(early[:, 2:4], *inner)
    far_second = [moved(early[:, 2], wrap), moved(early[:, 3], wrap)]
    late = exchange(late)
    first = attend(place, frame_reach, (early, 4), (early, 0), prior_first)
    first, late, prior_second, key_late, value_late = lax.optimization_barrier(
        (first, late, prior_second, key_late, value_late)
    )
    first = exchange(first)
    second = attend(place, frame_reach, (late, 0), (early, 2), prior_second, *far_second)
    first, second = lax.optimization_barrier((first, second))
    second = exchange(second)
    key_cache, value_cache = place_caches(place, key_main, key_late, value_main, value_late)
    second, key_cache, value_cache = lax.optimization_barrier((second, key_cache, value_cache))
    advanced = finish(gate_row, first, second, residual)
    return (advanced, key_cache, value_cache)


def solution(mesh):
    return jax.shard_map(
        shards,
        mesh=mesh,
        in_specs=(
            P(("queue", "head"), None),
            P(("queue", "head"), None),
            P(("queue", "head"), None),
            P(("queue", "head"), None),
            P(),
            P(),
            P(),
            P(),
            P(),
        ),
        out_specs=(
            P(("queue", "head"), None),
            P(("queue", "head"), None),
            P(("queue", "head"), None),
        ),
        check_vma=False,
    )
```

```python
import math

import jax
import jax.numpy as jnp
from jax import lax
from jax.experimental import pallas as pl
from jax.experimental.pallas import tpu as pltpu
from jax.sharding import PartitionSpec as P

HD = 128
FRAMES_GRP = 4
FRAME_SLOTS = 4
PREP_ROWS = 64
CACHE_PARTS = 4
QUERY_ROWS = 256
WRAP_TO = 8
KEY_RELAY, VALUE_RELAY = 3, 0
LOG2E = 1.4426950408889634
SMEM = pltpu.SMEM
VMEM_LIMIT = 60 * 1024 * 1024


def normalize(token_rows, gain_row):
    values = token_rows.astype(jnp.float32)
    square = jnp.mean(values * values, axis=-1, keepdims=True)
    return (values * lax.rsqrt(square + 1e-06) * gain_row).astype(jnp.bfloat16)


def prep_kernel(q_ref, k_ref, v_ref, qg_ref, kg_ref, early_ref, late_ref, key_ref):
    value = v_ref[...]
    key_norm = normalize(k_ref[...], kg_ref[...])
    query_norm = normalize(q_ref[...], qg_ref[...])
    key_ref[...] = key_norm
    for head in range(q_ref.shape[1] // HD):
        at = slice(head * HD, (head + 1) * HD)
        slot, second = head // 2, head % 2
        early_ref[slot, 2 * second] = value[:, at]
        early_ref[slot, 2 * second + 1] = key_norm[:, at]
        if second:
            late_ref[slot, 0] = query_norm[:, at]
        else:
            early_ref[slot, 4] = query_norm[:, at]


def prepare(queries, key_proj, value_proj, query_gain, key_gain):
    tok_dev, features = queries.shape
    slots = features // HD // 2
    row_block = pl.BlockSpec((PREP_ROWS, features), lambda i: (i, 0))
    gain_block = pl.BlockSpec((1, features), lambda i: (0, 0))
    return pl.pallas_call(
        prep_kernel,
        grid=(tok_dev // PREP_ROWS,),
        in_specs=[row_block, row_block, row_block, gain_block, gain_block],
        out_specs=[
            pl.BlockSpec((slots, 5, PREP_ROWS, HD), lambda i: (0, 0, i, 0)),
            pl.BlockSpec((slots, 1, PREP_ROWS, HD), lambda i: (0, 0, i, 0)),
            row_block,
        ],
        out_shape=[
            jax.ShapeDtypeStruct((slots, 5, tok_dev, HD), jnp.bfloat16),
            jax.ShapeDtypeStruct((slots, 1, tok_dev, HD), jnp.bfloat16),
            jax.ShapeDtypeStruct((tok_dev, features), jnp.bfloat16),
        ],
        compiler_params=pltpu.CompilerParams(vmem_limit_bytes=VMEM_LIMIT),
        cost_estimate=pl.CostEstimate(flops=8_000_000, bytes_accessed=8_000_000, transcendentals=0),
        name="prep",
    )(queries, key_proj, value_proj, query_gain.reshape(1, -1), key_gain.reshape(1, -1))


def attend_kernel(
    place_ref,
    reach_ref,
    query_ref,
    own_value,
    own_key,
    *refs,
):
    *priors, out_ref, total_ref, held_ref, sems = refs
    frame = pl.program_id(0)
    queue_pos = place_ref[0]
    main, *far = priors

    @pl.when((frame == 0) & ((queue_pos != WRAP_TO) | (not far)))
    def _():
        load = pltpu.make_async_copy(main, held_ref, sems.at[0])
        load.start()
        load.wait()

    if far:

        @pl.when((frame == 0) & (queue_pos == WRAP_TO))
        def _():
            loads = [
                pltpu.make_async_copy(part, held_ref.at[:, at], sems.at[at])
                for at, part in enumerate(far)
            ]
            for load in loads:
                load.start()
            for load in loads:
                load.wait()

    prior_value, prior_key = held_ref.at[:, 0], held_ref.at[:, 1]
    lowest = jnp.where(queue_pos > 0, -FRAMES_GRP, 0)
    lower = jnp.maximum(frame - reach_ref[queue_pos * FRAMES_GRP + frame], lowest)
    own_from = jnp.maximum(lower, 0)
    prior_from = jnp.minimum(lower, 0) + FRAMES_GRP
    rows = query_ref.shape[0] * query_ref.shape[1]
    scale = LOG2E / math.sqrt(HD)

    def scores_of(query, key):
        return lax.dot_general(
            query, key, (((1,), (1,)), ((), ())), preferred_element_type=jnp.float32
        )

    def block(ref, start, count):
        slots = ref[pl.ds(start * FRAME_SLOTS, count * FRAME_SLOTS)]
        return slots.reshape(count * rows, HD)

    def plain(parts):
        pairs = [
            (block(key_ref, start, FRAMES_GRP - start), block(value_ref, start, FRAMES_GRP - start))
            for key_ref, value_ref, start in parts
        ]
        query = query_ref[...].reshape(rows, HD)
        for low in range(0, rows, QUERY_ROWS):
            at = slice(low, low + QUERY_ROWS)
            lanes, mixed = None, None
            for key, value in pairs:
                weights = jnp.exp2(scores_of(query[at], key) * scale)
                part = jnp.dot(
                    weights.astype(jnp.bfloat16), value, preferred_element_type=jnp.float32
                )
                mixed = part if mixed is None else mixed + part
                for col in range(0, weights.shape[1], HD):
                    one = weights[:, col : col + HD]
                    lanes = one if lanes is None else lanes + one
            total = jnp.sum(lanes, axis=1, keepdims=True)
            slot = low // out_ref.shape[1]
            count = QUERY_ROWS // out_ref.shape[1]
            result = (mixed / total).astype(jnp.bfloat16)
            out_ref[slot : slot + count] = result.reshape(count, *out_ref.shape[1:])
            total_ref[at] = total

    for start in range(FRAMES_GRP):

        @pl.when((own_from == start) & (prior_from == FRAMES_GRP))
        def _(start=start):
            plain([(own_key, own_value, start)])

        @pl.when(prior_from == start)
        def _(start=start):
            plain([(own_key, own_value, 0), (prior_key, prior_value, start)])

    def store(mixed, total):
        out_ref[...] = (mixed / total).astype(jnp.bfloat16).reshape(out_ref.shape)

    total = total_ref[...]
    inside = (jnp.max(total) < 1e37) & (jnp.min(total) > 1e-25)

    @pl.when(jnp.logical_not(inside))
    def _():
        query = query_ref[...].reshape(rows, HD)

        def tile(key, value, carry):
            highest, total, mixed = carry
            scores = scores_of(query, key)
            raised = jnp.maximum(highest, jnp.max(scores, axis=1, keepdims=True))
            fade = jnp.exp2((highest - raised) * scale)
            weights = jnp.exp2((scores - raised) * scale)
            total = total * fade + jnp.sum(weights, axis=1, keepdims=True)
            part = jnp.dot(weights.astype(jnp.bfloat16), value, preferred_element_type=jnp.float32)
            return raised, total, mixed * fade + part

        def own_tile(step, carry):
            return tile(block(own_key, step, 1), block(own_value, step, 1), carry)

        def prior_tile(step, carry):
            return tile(block(prior_key, step, 1), block(prior_value, step, 1), carry)

        start = jnp.full((rows, 1), -1e30, jnp.float32)
        carry = (start, jnp.zeros_like(start), jnp.zeros((rows, HD), jnp.float32))
        carry = lax.fori_loop(own_from, FRAMES_GRP, own_tile, carry)
        _, total, mixed = lax.fori_loop(prior_from, FRAMES_GRP, prior_tile, carry)
        store(mixed, total)


def attend(place, frame_reach, query, own, *priors):
    query, query_at = query
    own, own_at = own
    slots, _, tok_dev, _ = own.shape
    rows = FRAME_SLOTS * tok_dev

    def whole(index):
        return pl.BlockSpec((slots, None, tok_dev, HD), lambda i: (0, index, 0, 0))

    return pl.pallas_call(
        attend_kernel,
        grid=(FRAMES_GRP,),
        in_specs=[
            pl.BlockSpec(memory_space=SMEM),
            pl.BlockSpec(memory_space=SMEM),
            pl.BlockSpec((FRAME_SLOTS, None, tok_dev, HD), lambda i: (i, query_at, 0, 0)),
            whole(own_at),
            whole(own_at + 1),
            pl.BlockSpec(memory_space=pl.ANY),
            *[pl.BlockSpec((slots, tok_dev, HD), lambda i: (0, 0, 0)) for _ in priors[1:]],
        ],
        out_specs=pl.BlockSpec((FRAME_SLOTS, tok_dev, HD), lambda i: (i, 0, 0)),
        out_shape=jax.ShapeDtypeStruct((slots, tok_dev, HD), jnp.bfloat16),
        scratch_shapes=[
            pltpu.VMEM((rows, 1), jnp.float32),
            pltpu.VMEM(priors[0].shape, jnp.bfloat16),
            pltpu.SemaphoreType.DMA((2,)),
        ],
        compiler_params=pltpu.CompilerParams(vmem_limit_bytes=VMEM_LIMIT),
        cost_estimate=pl.CostEstimate(
            flops=8_000_000_000, bytes_accessed=3_000_000, transcendentals=8_000_000
        ),
        name="attend",
    )(place, frame_reach, query, own, own, *priors)


def place_kernel(
    place_ref,
    key_main,
    key_late,
    value_main,
    value_late,
    key_out,
    value_out,
    key_held,
    value_held,
    sems,
):
    late = place_ref[0] == WRAP_TO
    rows = key_held.shape[0] // CACHE_PARTS
    for part in range(CACHE_PARTS):
        at = pl.ds(part * rows, rows)

        def load(source, held, index, at=at, part=part):
            return pltpu.make_async_copy(source.at[at], held.at[at], sems.at[index, part])

        @pl.when(late)
        def _(load=load):
            load(key_late, key_held, 0).start()
            load(value_late, value_held, 1).start()

        @pl.when(jnp.logical_not(late))
        def _(load=load):
            load(key_main, key_held, 0).start()
            load(value_main, value_held, 1).start()

    stores = []
    for part in range(CACHE_PARTS):
        at = pl.ds(part * rows, rows)
        for index, source, held, out in (
            (0, key_main, key_held, key_out),
            (1, value_main, value_held, value_out),
        ):
            pltpu.make_async_copy(source.at[at], held.at[at], sems.at[index, part]).wait()
            store = pltpu.make_async_copy(held.at[at], out.at[at], sems.at[index + 2, part])
            store.start()
            stores.append(store)
    for store in stores:
        store.wait()


def place_caches(place, key_main, key_late, value_main, value_late):
    anywhere = pl.BlockSpec(memory_space=pl.ANY)
    whole = jax.ShapeDtypeStruct(key_main.shape, jnp.bfloat16)
    return pl.pallas_call(
        place_kernel,
        in_specs=[pl.BlockSpec(memory_space=SMEM), anywhere, anywhere, anywhere, anywhere],
        out_specs=[anywhere, anywhere],
        out_shape=[whole, whole],
        scratch_shapes=[
            pltpu.VMEM(key_main.shape, jnp.bfloat16),
            pltpu.VMEM(key_main.shape, jnp.bfloat16),
            pltpu.SemaphoreType.DMA((4, CACHE_PARTS)),
        ],
        compiler_params=pltpu.CompilerParams(vmem_limit_bytes=VMEM_LIMIT),
        cost_estimate=pl.CostEstimate(flops=0, bytes_accessed=4_000_000, transcendentals=0),
        name="place_caches",
    )(place, key_main, key_late, value_main, value_late)


def finish_kernel(gate_ref, first_ref, second_ref, residual_ref, out_ref):
    for head in range(residual_ref.shape[1] // HD):
        source = second_ref if head % 2 else first_ref
        at = slice(head * HD, (head + 1) * HD)
        mixed = gate_ref[:, at] * source[head // 2].astype(jnp.float32)
        out_ref[:, at] = (residual_ref[:, at].astype(jnp.float32) + mixed).astype(jnp.bfloat16)


def finish(gate_row, first, second, residual):
    tok_dev, features = residual.shape
    blocks = 2
    wide = features // blocks
    row_block = pl.BlockSpec((tok_dev, wide), lambda i: (0, i))
    item_block = pl.BlockSpec((first.shape[0] // blocks, tok_dev, HD), lambda i: (i, 0, 0))
    return pl.pallas_call(
        finish_kernel,
        grid=(blocks,),
        in_specs=[
            pl.BlockSpec((1, wide), lambda i: (0, i)),
            item_block,
            item_block,
            row_block,
        ],
        out_specs=row_block,
        out_shape=jax.ShapeDtypeStruct(residual.shape, jnp.bfloat16),
        compiler_params=pltpu.CompilerParams(vmem_limit_bytes=VMEM_LIMIT),
        name="finish",
    )(gate_row, first, second, residual)


def moved(shard, *pairs):
    return lax.ppermute(shard, "queue", list(pairs))


def inner_pairs():
    return [(i, i + 1) for i in range(lax.axis_size("queue") - 1) if i + 1 != WRAP_TO]


def exchange(items):
    return lax.all_to_all(items, "head", split_axis=0, concat_axis=0, tiled=True)


def shards(
    queries,
    key_proj,
    value_proj,
    residual,
    query_gain,
    key_gain,
    gate_table,
    noise_level,
    frame_reach,
):
    queue_pos, head_pos = lax.axis_index("queue"), lax.axis_index("head")
    place = jnp.stack([queue_pos, head_pos]).astype(jnp.int32)
    frame = queue_pos * FRAMES_GRP + head_pos // FRAME_SLOTS
    level = lax.dynamic_index_in_dim(noise_level, frame, 0, keepdims=False)
    gate_row = lax.dynamic_slice_in_dim(gate_table, level, 1, 0)
    early, late, key_norm = prepare(queries, key_proj, value_proj, query_gain, key_gain)
    inner = inner_pairs()
    every = (*inner, (WRAP_TO - 1, WRAP_TO))
    value_main = moved(value_proj, *inner)
    key_main = moved(key_norm, *inner)
    value_half = moved(value_proj, (WRAP_TO - 1, VALUE_RELAY))
    key_half = moved(key_norm, (WRAP_TO - 1, KEY_RELAY))
    early = exchange(early)
    early, late, value_main, key_main, value_half, key_half, gate_row, place = (
        lax.optimization_barrier(
            (early, late, value_main, key_main, value_half, key_half, gate_row, place)
        )
    )
    key_late = moved(key_half, (KEY_RELAY, WRAP_TO))
    value_late = moved(value_half, (VALUE_RELAY, WRAP_TO))
    wrap = (WRAP_TO - 1, WRAP_TO)
    prior_first = moved(early[:, 0:2], *every)
    prior_second = moved(early[:, 2:4], *inner)
    far_second = [moved(early[:, 2], wrap), moved(early[:, 3], wrap)]
    late = exchange(late)
    first = attend(place, frame_reach, (early, 4), (early, 0), prior_first)
    first, late, prior_second, key_late, value_late = lax.optimization_barrier(
        (first, late, prior_second, key_late, value_late)
    )
    first = exchange(first)
    second = attend(place, frame_reach, (late, 0), (early, 2), prior_second, *far_second)
    first, second = lax.optimization_barrier((first, second))
    second = exchange(second)
    key_cache, value_cache = place_caches(place, key_main, key_late, value_main, value_late)
    second, key_cache, value_cache = lax.optimization_barrier((second, key_cache, value_cache))
    advanced = finish(gate_row, first, second, residual)
    return (advanced, key_cache, value_cache)


def solution(mesh):
    return jax.shard_map(
        shards,
        mesh=mesh,
        in_specs=(
            P(("queue", "head"), None),
            P(("queue", "head"), None),
            P(("queue", "head"), None),
            P(("queue", "head"), None),
            P(),
            P(),
            P(),
            P(),
            P(),
        ),
        out_specs=(
            P(("queue", "head"), None),
            P(("queue", "head"), None),
            P(("queue", "head"), None),
        ),
        check_vma=False,
    )
```
